768 devices in a mesh: dp: 48 (over z, y_hi, core), fsdp: 16 (over x, y_lo).
Axes of the slice: x: 4, y: 8 (y_hi: 2, y_lo: 4; y = y_hi * 4 + y_lo), z: 12, core: 2. Of those that a mesh axis runs over, the one named last changes fastest.
Arguments:
- acts: bfloat16 [196608, 4096], P(('dp', 'fsdp')), may hold values from -6 to 6
- cotangent: bfloat16 [196608, 4096], P(('dp', 'fsdp')), may hold values from -0.03125 to 0.03125
- projector: bfloat16 [4096, 512], P('fsdp'), may hold values from -0.09375 to 0.09375
- first_moment: float32 [4096, 512], P('fsdp'), may hold values from -4 to 4
- second_moment: float32 [4096, 512], P('fsdp'), may hold values from 0.0005 to 0.005
Outputs:
- first_new: float32 [4096, 512], P('fsdp')
- second_new: float32 [4096, 512], P('fsdp')
- update: float32 [4096, 4096], P(None, 'fsdp')
The draws below stay inside these ranges and needn't reach their ends.
All inputs are finite; a program needn't handle non-finite values.
Results may differ from the reference program's by a relative error of at most 0.017.
Values may be sent and summed in bfloat16 or wider, within the bound.
A program may use at most 64 MiB of HBM per device.

```python
import math
import jax
import jax.numpy as jnp
from jax import lax

D = 4096
RANK = 512
TOK_DEV = 256
STEP = 2
TOKENS = 196608


def levels(stream_key, dims, split, low, top_value):
    factor_of = 1.0
    for position, blocks in split:
        heights = jax.random.uniform(jax.random.fold_in(jax.random.fold_in(stream_key, 6), position), (blocks,), jnp.float32, low / len(split), top_value / len(split))
        factor_of = factor_of * jnp.repeat(jnp.exp(heights), dims[position] // blocks).reshape((-1,) + (1,) * (len(dims) - 1 - position))
    return factor_of


def scatter_about(own_key, shape, deviation, reach, cuts=(), dtype=jnp.bfloat16):
    loudness = levels(own_key, shape, cuts, -0.22, 0.18) if cuts else 1.0
    values = jax.random.normal(own_key, shape, jnp.float32) * deviation * loudness
    return jnp.minimum(jnp.maximum(values, -reach), reach).astype(dtype)


def setup_inputs(seed: int = 0) -> dict:
    seeds = jax.random.split(jax.random.key(seed), 6)
    return {
        "acts": scatter_about(seeds[0], (TOKENS, D), 1.0, 6.0, ((0, 768),)),
        "cotangent": scatter_about(seeds[1], (TOKENS, D), (TOKENS ** -0.5), 0.03125, ((0, 768),)),
        "projector": scatter_about(seeds[2], (D, RANK), D ** -0.5, 0.09375, ((0, 16),)),
        "first_moment": scatter_about(seeds[3], (D, RANK), 0.3, 4.0, ((0, 16),), jnp.float32),
        "second_moment": jnp.clip(jnp.exp(math.log(0.005) - 2.30258502 * jax.random.uniform(seeds[4], (D, RANK), jnp.float32) ** levels(seeds[4], (D, RANK), ((0, 16),), -0.2, 0.2)), 0.0005, 0.005),
    }


def reference(acts, cotangent, projector, first_moment, second_moment):
    blocks = TOKENS // TOK_DEV
    acts_blocks = acts.reshape(blocks, TOK_DEV, D)
    cot_blocks = cotangent.reshape(blocks, TOK_DEV, D)
    proj_wide = projector.astype(jnp.float32)

    def accumulate(total, pair):
        block_acts, block_cot = pair
        coords = jnp.dot(block_acts.astype(jnp.float32), proj_wide, preferred_element_type=jnp.float32).astype(jnp.bfloat16)
        term = jnp.dot(block_cot.astype(jnp.float32).T, coords.astype(jnp.float32), preferred_element_type=jnp.float32)
        term = lax.optimization_barrier(term.astype(jnp.bfloat16)).astype(jnp.float32)
        return (total + term, None)
    grad_low, _ = lax.scan(accumulate, jnp.zeros((D, RANK), jnp.float32), (acts_blocks, cot_blocks))
    first_new = 0.9 * first_moment + 0.1 * grad_low
    second_new = 0.999 * second_moment + 0.001 * grad_low * grad_low
    first_fix = 1.0 - 0.9 ** STEP
    second_fix = 1.0 - 0.999 ** STEP
    direction = (first_new / first_fix / (jnp.sqrt(second_new / second_fix) + 1e-08)).astype(jnp.bfloat16)
    update = lax.dot_general(projector, direction, (((1,), (1,)), ((), ())), preferred_element_type=jnp.float32)
    return (first_new, second_new, update)
```

```python
import jax
import jax.numpy as jnp
from jax import lax
from jax.experimental import pallas as pl
from jax.experimental.pallas import tpu as pltpu
from jax.sharding import PartitionSpec as P

MESH = pl.DeviceIdType.MESH
STEP = 2
NX, NY, NYL, NZ = 4, 8, 4, 12
BLK = 256
HALF, QUART = 128, 64
PIECE = 48
X, Y = 0, 1
BF16, F32 = jnp.bfloat16, jnp.float32


def gather_reduce(
    acts, cot, proj, pfull, gsum,
    acts_v, cot_v, p_v, acc, coords_t, term_v,
    far1, dir1, comb1, csrc1, mid_v, own2, far2, dir2, comb2, csrc2,
    zb, zrecv, ybuf, gb,
    ld_sem, sib_send, sib_recv, ag_send, ag_recv, out_sem, osib_send, osib_recv,
    rs_send, rs1_recv, rs2_recv, z_send, z_recv, y_sem, g_send, g_recv, fin_sem,
):
    dp, fs = lax.axis_index("dp"), lax.axis_index("fsdp")
    core, y_hi, z = dp % 2, (dp // 2) % 2, dp // 4
    x, y_lo = fs // NYL, fs % NYL
    y = y_hi * NYL + y_lo

    def device(dx=0, dy=0, dz=0, other=False):
        yy = (y + dy + NY) % NY
        xx = (x + dx + NX) % NX
        zz = (z + dz) % NZ
        cc = 1 - core if other else core
        return ((zz * 2 + yy // NYL) * 2 + cc, xx * NYL + yy % NYL)

    sibling = device(other=True)
    near = {(X, 1): device(dx=1), (X, -1): device(dx=-1), (Y, 1): device(dy=1), (Y, -1): device(dy=-1)}
    across = device(dy=4)
    column = [device(dz=k) for k in range(NZ)]
    mine = pl.ds(pl.multiple_of(core * BLK, BLK), BLK)

    def block_of(s):
        return ((x + s // 4) % NX) * NYL + (y_lo + s % 4) % NYL

    def columns(s):
        return pl.ds(pl.multiple_of(block_of(s) * BLK, BLK), BLK)

    own_p = pltpu.make_async_copy(proj.at[:, mine], p_v.at[0], ld_sem.at[2, 0])
    own_p.start()

    def load(s, _):
        pltpu.make_async_copy(acts.at[:, columns(s)], acts_v.at[s, pl.ds(0, BLK)], ld_sem.at[0, s]).start()
        pltpu.make_async_copy(cot.at[:, columns(s)], cot_v.at[s, pl.ds(0, BLK)], ld_sem.at[1, s]).start()
        return 0

    barrier = pltpu.get_barrier_semaphore()
    peers = [sibling, across, *near.values(), *column[1:]]
    for peer in peers:
        pl.semaphore_signal(barrier, inc=1, device_id=peer, device_id_type=MESH)
    lax.fori_loop(0, 16, load, 0)
    zb[pl.ds(512, 64), :] = jnp.zeros((64, 128), BF16)
    acc[...] = jnp.zeros_like(acc)
    pl.semaphore_wait(barrier, len(peers))

    def remote(src, dst, send, recv, target):
        copy = pltpu.make_async_remote_copy(
            src_ref=src, dst_ref=dst, send_sem=send, recv_sem=recv, device_id=target, device_id_type=MESH
        )
        copy.start()
        return copy

    def arrived(ref, sem):
        pltpu.make_async_copy(ref, ref, sem).wait()

    ag_sends = []

    def slot(part, u, v):
        return (u % 4) * 4 + v % 4 if part == 0 else (v % 4) * 4 + u % 4

    def rows(part, half):
        if half is None:
            return pl.ds(part * HALF, HALF)
        return pl.ds(part * HALF + half * QUART, QUART)

    def spread(part, u, v, half, stage, way):
        axis = (X, Y)[part] if stage == 1 else (Y, X)[part]
        s = slot(part, u, v)
        d = slot(part, u - way, v) if stage == 1 else slot(part, u, v - way)
        r = rows(part, half)
        src = proj.at[r, mine] if s == 0 else p_v.at[s, r]
        ag_sends.append(
            remote(
                src, p_v.at[d, r], ag_send.at[len(ag_sends)], ag_recv.at[part, d, half or 0], near[axis, way]
            )
        )

    seen = set()

    def got(part, u, v, half=None):
        s = slot(part, u, v)
        if (part, s, half) not in seen:
            seen.add((part, s, half))
            arrived(p_v.at[s, rows(part, half)], ag_recv.at[part, s, half or 0])

    def gotten(part, u, v):
        if v % 4 == 2:
            got(part, u, v, 0)
            got(part, u, v, 1)
        elif v % 4 != 0:
            got(part, u, v)
        elif u % 4 == 2:
            got(part, u, v, 0)
            got(part, u, v, 1)
        elif u % 4 != 0:
            got(part, u, v)

    def multiply(rx, ry):
        s = (rx % 4) * 4 + ry % 4
        gotten(0, rx, ry)
        gotten(1, ry, rx)
        arrived(acts_v.at[s, pl.ds(0, BLK)], ld_sem.at[0, s])
        arrived(acts_v.at[s, pl.ds(BLK, BLK)], sib_recv.at[0, s])
        acc[...] += jnp.dot(acts_v[s], p_v[s], preferred_element_type=F32)

    for part in (0, 1):
        for stage in (1, 2):
            for way in (1, -1):
                spread(part, 0, 0, None, stage, way)

    def lend(s, _):
        remote(acts.at[:, columns(s)], acts_v.at[s, pl.ds(BLK, BLK)], sib_send.at[0, s], sib_recv.at[0, s], sibling)
        return 0

    def lend_cot(s, _):
        remote(cot.at[:, columns(s)], cot_v.at[s, pl.ds(BLK, BLK)], sib_send.at[1, s], sib_recv.at[1, s], sibling)
        return 0

    lax.fori_loop(0, 16, lend, 0)
    lax.fori_loop(0, 16, lend_cot, 0)
    own_p.wait()

    def relay(part, u):
        gotten(part, u, 3)
        spread(part, u, 3, 0, 2, 1)
        gotten(part, u, 1)
        spread(part, u, 1, 1, 2, -1)

    for part in (0, 1):
        gotten(part, 3, 0)
        spread(part, 3, 0, 0, 1, 1)
        gotten(part, 1, 0)
        spread(part, 1, 0, 1, 1, -1)
    for part in (0, 1):
        for u in (3, 1):
            spread(part, u, 0, None, 2, 1)
            spread(part, u, 0, None, 2, -1)
    for part in (0, 1):
        relay(part, 0)
    multiply(0, 0)
    for part in (0, 1):
        gotten(part, 2, 0)
        spread(part, 2, 0, None, 2, 1)
        spread(part, 2, 0, None, 2, -1)
    for rx, ry in ((1, 0), (3, 0), (0, 1), (0, 3)):
        multiply(rx, ry)
    for u in (3, 1):
        for part in (0, 1):
            relay(part, u)
    for rx, ry in ((1, 1), (1, 3), (3, 1), (3, 3)):
        multiply(rx, ry)
    for part in (0, 1):
        relay(part, 2)
    for rx, ry in ((2, 0), (0, 2), (1, 2), (3, 2), (2, 1), (2, 3), (2, 2)):
        multiply(rx, ry)

    def give(s, _):
        place = pl.ds(pl.multiple_of(block_of(s) * BLK, BLK), BLK)
        pltpu.make_async_copy(p_v.at[s], pfull.at[core, place], out_sem.at[s]).start()
        remote(p_v.at[s], pfull.at[core, place], osib_send.at[s], osib_recv.at[s], sibling)
        return 0

    coords_t[...] = acc[...].astype(BF16).T

    rs_sends = []

    def send(src, dst, sem, axis, way):
        rs_sends.append(remote(src, dst, rs_send.at[len(rs_sends)], sem, near[axis, way]))

    def rs_slot(part, u, v):
        return (v % 4) * 4 + u % 4 if part == 0 else (u % 4) * 4 + v % 4

    def term(s):
        arrived(cot_v.at[s, pl.ds(0, BLK)], ld_sem.at[1, s])
        arrived(cot_v.at[s, pl.ds(BLK, BLK)], sib_recv.at[1, s])
        term_v[s] = jnp.dot(coords_t[...], cot_v[s], preferred_element_type=F32).astype(BF16)

    first = ((Y, X), (X, Y))
    WAYS = ((0, 1), (1, -1))
    done = set()

    def need(part, u, v):
        s = rs_slot(part, u, v)
        if s not in done:
            done.add(s)
            term(s)
        return s

    order = (2, 1, 3, 0)
    for v in order:
        for part in (0, 1):
            s = need(part, 2, v)
            for w, way in WAYS:
                send(term_v.at[s, rows(part, w)], far1.at[part, w, v], rs1_recv.at[0, part, w, v], first[part][0], way)
    for v in order:
        for part in (0, 1):
            for w, way in WAYS:
                s = need(part, way, v)
                send(
                    term_v.at[s, rows(part, 1 - w)], dir1.at[part, w, v], rs1_recv.at[1, part, w, v],
                    first[part][0], way,
                )
    need(0, 0, 0)
    for v in order:
        for part in (0, 1):
            for w, way in WAYS:
                s = rs_slot(part, way, v)
                arrived(far1.at[part, w, v], rs1_recv.at[0, part, w, v])
                csrc1[part, w, v] = (
                    term_v[s, rows(part, w), :].astype(F32) + far1[part, w, v].astype(F32)
                ).astype(BF16)
                send(csrc1.at[part, w, v], comb1.at[part, w, v], rs1_recv.at[2, part, w, v], first[part][0], way)
    lax.fori_loop(0, 16, give, 0)

    def total1(part, v, w):
        s = rs_slot(part, 0, v)
        arrived(comb1.at[part, w, v], rs1_recv.at[2, part, w, v])
        arrived(dir1.at[part, 1 - w, v], rs1_recv.at[1, part, 1 - w, v])
        return (
            term_v[s, rows(part, w), :].astype(F32)
            + comb1[part, w, v].astype(F32)
            + dir1[part, 1 - w, v].astype(F32)
        )

    for v in (2, 1, 3):
        for part in (0, 1):
            for w, way in WAYS:
                mid_v[part, v, pl.ds(w * QUART, QUART), :] = total1(part, v, w).astype(BF16)
                if v == 2:
                    send(
                        mid_v.at[part, v, pl.ds(w * QUART, QUART)], far2.at[part, w], rs2_recv.at[0, part, w],
                        first[part][1], way,
                    )
                elif v % 4 == (-way) % 4:
                    send(
                        mid_v.at[part, v, pl.ds(w * QUART, QUART)], dir2.at[part, 1 - w], rs2_recv.at[1, part, 1 - w],
                        first[part][1], -way,
                    )
    for part in (0, 1):
        for w, way in WAYS:
            own2[part, pl.ds(w * QUART, QUART), :] = total1(part, 0, w)
    for part in (0, 1):
        for w, way in WAYS:
            arrived(far2.at[part, w], rs2_recv.at[0, part, w])
            csrc2[part, w] = (
                mid_v[part, way % 4, pl.ds(w * QUART, QUART), :].astype(F32) + far2[part, w].astype(F32)
            ).astype(BF16)
            send(csrc2.at[part, w], comb2.at[part, w], rs2_recv.at[2, part, w], first[part][1], way)
    for part in (0, 1):
        for w, way in WAYS:
            arrived(comb2.at[part, w], rs2_recv.at[2, part, w])
            arrived(dir2.at[part, 1 - w], rs2_recv.at[1, part, 1 - w])
            total = (
                own2[part, pl.ds(w * QUART, QUART), :]
                + comb2[part, w].astype(F32)
                + dir2[part, 1 - w].astype(F32)
            ).astype(BF16)
            at = part * HALF + w * QUART
            zb[pl.ds(at, QUART), :] = total[:, :128]
            zb[pl.ds(256 + at, QUART), :] = total[:, 128:]

    def piece(k):
        return pl.ds(pl.multiple_of(((z + k) % NZ) * PIECE, 16), PIECE)

    far_first = (6, 5, 7, 4, 8, 3, 9, 2, 10, 1, 11)
    out = [
        remote(zb.at[piece(k)], zrecv.at[k], z_send.at[k], z_recv.at[k], column[k]) for k in far_first
    ]
    part_sum = zb[piece(0), :].astype(F32)
    for k in reversed(far_first):
        arrived(zrecv.at[k], z_recv.at[k])
        part_sum += zrecv[k].astype(F32)
    ybuf[0] = part_sum.astype(BF16)
    swap = remote(ybuf.at[0], ybuf.at[1], y_sem.at[0], y_sem.at[1], across)
    swap.wait()
    gb[piece(0), :] = (ybuf[0].astype(F32) + ybuf[1].astype(F32)).astype(BF16)
    back = [
        remote(gb.at[piece(0)], gb.at[piece(0)], g_send.at[k], g_recv.at[k], column[k]) for k in far_first
    ]
    for k in reversed(far_first):
        arrived(gb.at[piece(NZ - k)], g_recv.at[k])
    keep = pltpu.make_async_copy(gb, gsum.at[core], fin_sem.at[0])
    keep.start()
    tell = remote(gb, gsum.at[core], fin_sem.at[1], fin_sem.at[2], sibling)

    def finish(s, _):
        other = 1 - core
        place = pl.ds(pl.multiple_of(block_of(s) * BLK, BLK), BLK)
        arrived(acts_v.at[s, pl.ds(0, BLK)], sib_send.at[0, s])
        arrived(cot_v.at[s, pl.ds(0, BLK)], sib_send.at[1, s])
        arrived(pfull.at[core, place], out_sem.at[s])
        arrived(p_v.at[s], osib_send.at[s])
        arrived(pfull.at[other, place], osib_recv.at[s])
        return 0

    lax.fori_loop(0, 16, finish, 0)
    for copy in ag_sends + rs_sends + out + back:
        copy.wait_send()
    keep.wait()
    tell.wait_send()
    arrived(gsum.at[1 - core], fin_sem.at[2])


def gather_and_sum(acts, cotangent, projector):
    dma = pltpu.SemaphoreType.DMA
    any_space = pl.BlockSpec(memory_space=pl.ANY)
    return pl.pallas_call(
        gather_reduce,
        out_shape=(
            jax.ShapeDtypeStruct((2, 4096, BLK), BF16),
            jax.ShapeDtypeStruct((2, NZ * PIECE, 128), BF16),
        ),
        in_specs=[any_space] * 3,
        out_specs=(any_space, any_space),
        scratch_shapes=[
            pltpu.VMEM((16, 512, BLK), BF16),
            pltpu.VMEM((16, 512, BLK), BF16),
            pltpu.VMEM((16, BLK, BLK), BF16),
            pltpu.VMEM((512, BLK), F32),
            pltpu.VMEM((BLK, 512), BF16),
            pltpu.VMEM((16, BLK, BLK), BF16),
            pltpu.VMEM((2, 2, 4, QUART, BLK), BF16),
            pltpu.VMEM((2, 2, 4, QUART, BLK), BF16),
            pltpu.VMEM((2, 2, 4, QUART, BLK), BF16),
            pltpu.VMEM((2, 2, 4, QUART, BLK), BF16),
            pltpu.VMEM((2, 4, HALF, BLK), BF16),
            pltpu.VMEM((2, HALF, BLK), F32),
            pltpu.VMEM((2, 2, QUART, BLK), BF16),
            pltpu.VMEM((2, 2, QUART, BLK), BF16),
            pltpu.VMEM((2, 2, QUART, BLK), BF16),
            pltpu.VMEM((2, 2, QUART, BLK), BF16),
            pltpu.VMEM((NZ * PIECE, 128), BF16),
            pltpu.VMEM((NZ, PIECE, 128), BF16),
            pltpu.VMEM((2, PIECE, 128), BF16),
            pltpu.VMEM((NZ * PIECE, 128), BF16),
            dma((3, 16)),
            dma((2, 16)),
            dma((2, 16)),
            dma((48,)),
            dma((2, 16, 2)),
            dma((16,)),
            dma((16,)),
            dma((16,)),
            dma((64,)),
            dma((3, 2, 2, 4)),
            dma((3, 2, 2)),
            dma((NZ,)),
            dma((NZ,)),
            dma((2,)),
            dma((NZ,)),
            dma((NZ,)),
            dma((3,)),
        ],
        compiler_params=pltpu.CompilerParams(
            collective_id=1, has_side_effects=True, vmem_limit_bytes=40 << 20
        ),
        name="gather_and_sum",
    )(acts, cotangent, projector)


def update_kernel(p, g, m1, m2, first_new, second_new, update, direction):
    @pl.when(pl.program_id(0) == 0)
    def _():
        first_fix = 1.0 - 0.9**STEP
        second_fix = 1.0 - 0.999**STEP
        for half in range(2):
            low = jnp.concatenate(
                [g[half, pl.ds(0, 256), :], g[half, pl.ds(256, 256), :]], axis=1
            ).astype(F32).T
            cols = pl.ds(half * BLK, BLK)
            first = 0.9 * m1[:, cols] + 0.1 * low
            second = 0.999 * m2[:, cols] + 0.001 * low * low
            first_new[:, cols] = first
            second_new[:, cols] = second
            direction[half] = (
                first / first_fix / (jnp.sqrt(second / second_fix) + 1e-08)
            ).astype(BF16)

    dims = (((1,), (1,)), ((), ()))
    update[...] = lax.dot_general(
        p[0], direction[0], dims, preferred_element_type=F32
    ) + lax.dot_general(p[1], direction[1], dims, preferred_element_type=F32)


def adam_and_update(pfull, gsum, first_moment, second_moment):
    tile = 512
    whole = pl.BlockSpec((BLK, 512), lambda i: (0, 0))
    return pl.pallas_call(
        update_kernel,
        grid=(4096 // tile,),
        out_shape=(
            jax.ShapeDtypeStruct((BLK, 512), F32),
            jax.ShapeDtypeStruct((BLK, 512), F32),
            jax.ShapeDtypeStruct((4096, BLK), F32),
        ),
        in_specs=[
            pl.BlockSpec((2, tile, BLK), lambda i: (0, i, 0)),
            pl.BlockSpec((2, NZ * PIECE, 128), lambda i: (0, 0, 0)),
            whole,
            whole,
        ],
        out_specs=(whole, whole, pl.BlockSpec((tile, BLK), lambda i: (i, 0))),
        scratch_shapes=[pltpu.VMEM((2, BLK, BLK), BF16)],
        compiler_params=pltpu.CompilerParams(vmem_limit_bytes=32 << 20),
        name="adam_and_update",
    )(pfull, gsum, first_moment, second_moment)


def on_device(acts, cotangent, projector, first_moment, second_moment):
    pfull, gsum = gather_and_sum(acts, cotangent, projector)
    return adam_and_update(pfull, gsum, first_moment, second_moment)


def solution(mesh):
    in_specs = (
        P(("dp", "fsdp"), None),
        P(("dp", "fsdp"), None),
        P("fsdp", None),
        P("fsdp", None),
        P("fsdp", None),
    )
    out_specs = (P("fsdp", None), P("fsdp", None), P(None, "fsdp"))
    return jax.shard_map(
        on_device, mesh=mesh, in_specs=in_specs, out_specs=out_specs, check_vma=False
    )
```

```python
import jax
import jax.numpy as jnp
from jax import lax
from jax.experimental import pallas as pl
from jax.experimental.pallas import tpu as pltpu
from jax.sharding import PartitionSpec as P

MESH = pl.DeviceIdType.MESH
STEP = 2
NX, NY, NYL, NZ = 4, 8, 4, 12
BLK = 256
HALF, QUART = 128, 64
X, Y = 0, 1
BF16, F32 = jnp.bfloat16, jnp.float32


def gather_reduce(
    acts, cot, proj, p_v, g_big, g_small,
    acts_v, cot_v, acc, coords_t, term_v,
    far1a, dir1a, comb1a, csrc1a, mid_a, own2a, far2a, dir2a, comb2a, csrc2a, zb_a, zrecv_a, ybuf_a,
    far1b, dir1b, comb1b, csrc1b, mid_b, own2b, far2b, dir2b, comb2b, csrc2b, zb_b, zrecv_b, ybuf_b,
    hello, ld_sem, sib_send, sib_recv, ag_send, ag_recv, osib_sem,
    rs_send, rs_recv, z_sem, y_sem, g_sem, fin_sem,
):
    dp, fs = lax.axis_index("dp"), lax.axis_index("fsdp")
    core, y_hi, z = dp % 2, (dp // 2) % 2, dp // 4
    x, y_lo = fs // NYL, fs % NYL
    y = y_hi * NYL + y_lo

    def device(dx=0, dy=0, dz=0, other=False):
        yy = (y + dy + NY) % NY
        xx = (x + dx + NX) % NX
        zz = (z + dz) % NZ
        cc = 1 - core if other else core
        return ((zz * 2 + yy // NYL) * 2 + cc, xx * NYL + yy % NYL)

    sibling = device(other=True)
    near = {(X, 1): device(dx=1), (X, -1): device(dx=-1), (Y, 1): device(dy=1), (Y, -1): device(dy=-1)}
    across = device(dy=4)
    column = [device(dz=k) for k in range(NZ)]
    mine = pl.ds(pl.multiple_of(core * BLK, BLK), BLK)

    def columns(s):
        block = ((x + s // 4) % NX) * NYL + (y_lo + s % 4) % NYL
        return pl.ds(pl.multiple_of(block * BLK, BLK), BLK)

    def load(s, _):
        pltpu.make_async_copy(acts.at[:, columns(s)], acts_v.at[s, pl.ds(0, BLK)], ld_sem.at[0]).start()
        pltpu.make_async_copy(cot.at[:, columns(s)], cot_v.at[s, pl.ds(0, BLK)], ld_sem.at[1]).start()
        return 0

    barrier = pltpu.get_barrier_semaphore()
    peers = [*near.values(), column[1], column[NZ - 1], sibling]
    for peer in peers:
        pl.semaphore_signal(barrier, inc=1, device_id=peer, device_id_type=MESH)
    own_p = pltpu.make_async_copy(proj.at[:, mine], p_v.at[0, 0], ld_sem.at[2])
    own_p.start()
    lax.fori_loop(0, 16, load, 0)
    acc[...] = jnp.zeros_like(acc)
    pl.semaphore_wait(barrier, len(peers))

    chain = [near[Y, 1], near[Y, -1], column[1], column[NZ - 1]]

    def greet(r):
        if r > 0:
            pl.semaphore_wait(hello.at[r - 1], len(chain))
        if r < 5:
            for peer in chain:
                pl.semaphore_signal(hello.at[r], inc=1, device_id=peer, device_id_type=MESH)

    def remote(src, dst, send, recv, target):
        copy = pltpu.make_async_remote_copy(
            src_ref=src, dst_ref=dst, send_sem=send, recv_sem=recv, device_id=target, device_id_type=MESH
        )
        copy.start()
        return copy

    def arrived(ref, sem):
        pltpu.make_async_copy(ref, ref, sem).wait()

    both = (3, 0), (1, 0), (2, 0), (0, 3), (0, 1), (3, 3), (3, 1), (1, 3), (1, 1), (2, 3), (2, 1)

    def group(u, v):
        u, v = u % 4, v % 4
        return both.index((u, v)) if (u, v) in both else len(both) + (u == 2)

    def slot(part, u, v):
        return (u % 4) * 4 + v % 4 if part == 0 else (v % 4) * 4 + u % 4

    def rows(part, half):
        if half is None:
            return pl.ds(part * HALF, HALF)
        return pl.ds(part * HALF + half * QUART, QUART)

    def spread(part, u, v, half, stage, way):
        axis = (X, Y)[part] if stage == 1 else (Y, X)[part]
        s = slot(part, u, v)
        d = slot(part, u - way, v) if stage == 1 else slot(part, u, v - way)
        r = rows(part, half)
        src = proj.at[r, mine] if s == 0 else p_v.at[0, s, r]
        at = (u - way, v) if stage == 1 else (u, v - way)
        remote(src, p_v.at[0, d, r], ag_send.at[0], ag_recv.at[group(*at)], near[axis, way])

    seen = set()

    def gotten(u, v):
        if (u % 4, v % 4) == (0, 0):
            return
        g = group(u, v)
        if g not in seen:
            seen.add(g)
            arrived(p_v.at[0, pl.ds(0, 3 if g == len(both) else 1)], ag_recv.at[g])

    def multiply(rx, ry):
        s = (rx % 4) * 4 + ry % 4
        gotten(rx, ry)
        gotten(ry, rx)
        acc[...] += jnp.dot(acts_v[s], p_v[0, s], preferred_element_type=F32)

    for part in (0, 1):
        for way in (1, -1):
            spread(part, 0, 0, None, 1, way)
    for part in (0, 1):
        for way in (1, -1):
            spread(part, 0, 0, None, 2, way)
    greet(0)

    def lend(s, _):
        remote(acts.at[:, columns(s)], acts_v.at[s, pl.ds(BLK, BLK)], sib_send.at[0], sib_recv.at[0], sibling)
        return 0

    def lend_cot(s, _):
        remote(cot.at[:, columns(s)], cot_v.at[s, pl.ds(BLK, BLK)], sib_send.at[1], sib_recv.at[1], sibling)
        return 0

    def give(s, _):
        remote(p_v.at[0, s], p_v.at[1, s], osib_sem.at[0], osib_sem.at[1], sibling)
        return 0

    lax.fori_loop(0, 16, lend, 0)
    own_p.wait()

    def relay(part, u):
        gotten(u, 3)
        spread(part, u, 3, 0, 2, 1)
        gotten(u, 1)
        spread(part, u, 1, 1, 2, -1)

    for part in (0, 1):
        gotten(3, 0)
        spread(part, 3, 0, 0, 1, 1)
        gotten(1, 0)
        spread(part, 1, 0, 1, 1, -1)
    for part in (0, 1):
        for u in (3, 1):
            spread(part, u, 0, None, 2, 1)
            spread(part, u, 0, None, 2, -1)
    lax.fori_loop(0, 16, lend_cot, 0)
    for part in (0, 1):
        relay(part, 0)
    greet(1)
    arrived(acts_v.at[:, pl.ds(0, BLK)], ld_sem.at[0])
    arrived(acts_v.at[:, pl.ds(BLK, BLK)], sib_recv.at[0])
    multiply(0, 0)
    for part in (0, 1):
        gotten(2, 0)
        spread(part, 2, 0, None, 2, 1)
        spread(part, 2, 0, None, 2, -1)
    greet(2)
    for rx, ry in ((1, 0), (3, 0), (0, 1), (0, 3)):
        multiply(rx, ry)
    for u in (3, 1):
        for part in (0, 1):
            relay(part, u)
    greet(3)
    for rx, ry in ((2, 0), (0, 2), (1, 1), (1, 3), (3, 1), (3, 3)):
        multiply(rx, ry)
    for part in (0, 1):
        relay(part, 2)
    greet(4)
    for rx, ry in ((1, 2), (3, 2), (2, 1), (2, 3), (2, 2)):
        multiply(rx, ry)

    coords_t[...] = acc[...].astype(BF16).T
    arrived(cot_v.at[:, pl.ds(0, BLK)], ld_sem.at[1])
    arrived(cot_v.at[:, pl.ds(BLK, BLK)], sib_recv.at[1])

    first = ((Y, X), (X, Y))
    WAYS = ((0, 1), (1, -1))
    order = (2, 1, 3, 0)

    def rs_slot(part, u, v):
        return (v % 4) * 4 + u % 4 if part == 0 else (u % 4) * 4 + v % 4

    done = set()

    def need(part, u, v):
        s = rs_slot(part, u, v)
        if s not in done:
            done.add(s)
            term_v[s] = jnp.dot(coords_t[...], cot_v[s], preferred_element_type=F32).astype(BF16)
        return s

    class Run:
        def __init__(self, index, low, q, buffers):
            self.index, self.low, self.q, self.seen = index, low, q, set()
            (
                self.far1, self.dir1, self.comb1, self.csrc1, self.mid, self.own2,
                self.far2, self.dir2, self.comb2, self.csrc2, self.zb, self.zrecv, self.ybuf,
            ) = buffers

        def send(self, src, dst, kind, v, axis, way):
            recv = rs_recv.at[self.index, kind * 4 + v if kind < 3 else 9 + kind]
            remote(src, dst, rs_send.at[self.index, kind], recv, near[axis, way])

        def came(self, kind, v=None):
            if (kind, v) in self.seen:
                return
            self.seen.add((kind, v))
            buffer = (self.far1, self.dir1, self.comb1, self.far2, self.dir2, self.comb2)[kind]
            if kind < 3:
                arrived(buffer.at[:, :, v], rs_recv.at[self.index, kind * 4 + v])
            else:
                arrived(buffer, rs_recv.at[self.index, 9 + kind])

        def rows(self, part, half):
            return pl.ds(self.low + (2 * part + half) * self.q, self.q)

        def half(self, w):
            return pl.ds(w * self.q, self.q)

        def far(self):
            for v in order:
                for part in (0, 1):
                    s = need(part, 2, v)
                    for w, way in WAYS:
                        self.send(
                            term_v.at[s, self.rows(part, w)], self.far1.at[part, w, v],
                            0, v, first[part][0], way,
                        )

        def direct(self):
            for v in order:
                for part in (0, 1):
                    for w, way in WAYS:
                        s = need(part, way, v)
                        self.send(
                            term_v.at[s, self.rows(part, 1 - w)], self.dir1.at[part, w, v],
                            1, v, first[part][0], way,
                        )

        def combine(self):
            for v in order:
                for part in (0, 1):
                    for w, way in WAYS:
                        s = rs_slot(part, way, v)
                        self.came(0, v)
                        self.csrc1[part, w, v] = (
                            term_v[s, self.rows(part, w), :].astype(F32) + self.far1[part, w, v].astype(F32)
                        ).astype(BF16)
                        self.send(
                            self.csrc1.at[part, w, v], self.comb1.at[part, w, v],
                            2, v, first[part][0], way,
                        )

        def total1(self, part, v, w):
            s = rs_slot(part, 0, v)
            self.came(2, v)
            self.came(1, v)
            return (
                term_v[s, self.rows(part, w), :].astype(F32)
                + self.comb1[part, w, v].astype(F32)
                + self.dir1[part, 1 - w, v].astype(F32)
            )

        def middle(self):
            for v in (2, 1, 3):
                for part in (0, 1):
                    for w, way in WAYS:
                        self.mid[part, v, self.half(w), :] = self.total1(part, v, w).astype(BF16)
                        src = self.mid.at[part, v, self.half(w)]
                        if v == 2:
                            self.send(
                                src, self.far2.at[part, w], 3, 0, first[part][1], way
                            )
                        elif v % 4 == (-way) % 4:
                            self.send(
                                src, self.dir2.at[part, 1 - w], 4, 0, first[part][1], -way
                            )

        def own(self):
            for part in (0, 1):
                for w, _ in WAYS:
                    self.own2[part, self.half(w), :] = self.total1(part, 0, w)

        def combine2(self):
            for part in (0, 1):
                for w, way in WAYS:
                    self.came(3)
                    self.csrc2[part, w] = (
                        self.mid[part, way % 4, self.half(w), :].astype(F32) + self.far2[part, w].astype(F32)
                    ).astype(BF16)
                    self.send(
                        self.csrc2.at[part, w], self.comb2.at[part, w], 5, 0, first[part][1], way
                    )

        def total2(self):
            for part in (0, 1):
                for w, _ in WAYS:
                    self.came(5)
                    self.came(4)
                    total = (
                        self.own2[part, self.half(w), :]
                        + self.comb2[part, w].astype(F32)
                        + self.dir2[part, 1 - w].astype(F32)
                    ).astype(BF16)
                    at = (2 * part + w) * self.q
                    if self.index == 0:
                        self.zb[pl.ds(at, self.q), :] = total
                    else:
                        self.zb[pl.ds(at, self.q), :] = total[:, :128]
                        self.zb[pl.ds(64 + at, self.q), :] = total[:, 128:]

    big = Run(
        0, 0, 48,
        (far1a, dir1a, comb1a, csrc1a, mid_a, own2a, far2a, dir2a, comb2a, csrc2a, zb_a, zrecv_a, ybuf_a),
    )
    small = Run(
        1, 192, 16,
        (far1b, dir1b, comb1b, csrc1b, mid_b, own2b, far2b, dir2b, comb2b, csrc2b, zb_b, zrecv_b, ybuf_b),
    )

    far_first = (6, 5, 7, 4, 8, 3, 9, 2, 10, 1, 11)

    def piece(run, k):
        index = (z + k) % NZ if run.index == 0 else (z + k + 4) % NZ
        return pl.ds(pl.multiple_of(index * 16, 16), 16), index

    def owned(run, k, body):
        if run.index == 0:
            body()
        else:
            pl.when((z + k + 4) % NZ < 8)(body)

    def scatter(run):
        for k in far_first:

            def body(k=k):
                at, _ = piece(run, k)
                remote(run.zb.at[at], run.zrecv.at[k], z_sem.at[run.index, 0], z_sem.at[run.index, 1], column[k])

            owned(run, k, body)

    def swap(run):
        def body():
            at, _ = piece(run, 0)
            part_sum = run.zb[at, :].astype(F32)
            arrived(run.zrecv.at[pl.ds(1, NZ - 1)], z_sem.at[run.index, 1])
            for k in range(1, NZ):
                part_sum += run.zrecv[k].astype(F32)
            run.ybuf[0] = part_sum.astype(BF16)
            remote(run.ybuf.at[0], run.ybuf.at[1], y_sem.at[run.index, 0], y_sem.at[run.index, 1], across)

        owned(run, 0, body)

    def hand_out(run, result):
        def body():
            at, _ = piece(run, 0)
            arrived(run.ybuf.at[1], y_sem.at[run.index, 1])
            result[0, at, :] = (run.ybuf[0].astype(F32) + run.ybuf[1].astype(F32)).astype(BF16)
            for k in far_first:
                remote(result.at[0, at], result.at[0, at], g_sem.at[run.index, 0], g_sem.at[run.index, 1], column[k])

        owned(run, 0, body)

    def others(run, body):
        if run.index == 0:
            body(NZ - 1)
        else:
            pl.when((z + 4) % NZ < 8)(lambda: body(7))
            pl.when((z + 4) % NZ >= 8)(lambda: body(8))

    def collect(run, result):
        others(run, lambda n: arrived(run.zrecv.at[pl.ds(0, n)], g_sem.at[run.index, 1]))
        return remote(
            result.at[0], result.at[1], fin_sem.at[run.index, 0], fin_sem.at[run.index, 1], sibling
        )

    big.far()
    big.direct()
    need(0, 0, 0)
    small.far()
    big.combine()
    small.direct()
    greet(5)
    big.middle()
    small.combine()
    big.own()
    big.combine2()
    lax.fori_loop(0, 16, give, 0)
    small.middle()
    big.total2()
    scatter(big)
    small.own()
    small.combine2()
    small.total2()
    scatter(small)
    swap(big)
    swap(small)
    hand_out(big, g_big)
    hand_out(small, g_small)
    tell = [collect(big, g_big), collect(small, g_small)]

    arrived(acts_v.at[:, pl.ds(0, BLK)], sib_send.at[0])
    arrived(cot_v.at[:, pl.ds(0, BLK)], sib_send.at[1])
    arrived(p_v.at[0], osib_sem.at[0])
    arrived(p_v.at[1], osib_sem.at[1])
    arrived(p_v.at[0, pl.ds(0, 15)], ag_send.at[0])
    for run in (big, small):
        for kind, buffer in enumerate((run.far1, run.dir1, run.comb1, run.far2, run.dir2, run.comb2)):
            arrived(buffer, rs_send.at[run.index, kind])
        others(run, lambda n, run=run: arrived(run.zrecv.at[pl.ds(0, n)], z_sem.at[run.index, 0]))

        def body(run=run):
            arrived(run.ybuf.at[0], y_sem.at[run.index, 0])
            arrived(run.zrecv.at[pl.ds(0, NZ - 1)], g_sem.at[run.index, 0])

        owned(run, 0, body)
    for copy in tell:
        copy.wait()


def gather_and_sum(acts, cotangent, projector):
    dma = pltpu.SemaphoreType.DMA
    hbm = pl.BlockSpec(memory_space=pltpu.HBM)
    vmem = pl.BlockSpec(memory_space=pltpu.VMEM)

    def run_buffers(q, cols, pieces):
        first_stage = [pltpu.VMEM((2, 2, 4, q, BLK), BF16)] * 4
        second_stage = [pltpu.VMEM((2, 2, q, BLK), BF16)] * 4
        return [
            *first_stage,
            pltpu.VMEM((2, 4, 2 * q, BLK), BF16),
            pltpu.VMEM((2, 2 * q, BLK), F32),
            *second_stage,
            pltpu.VMEM((pieces * 16, cols), BF16),
            pltpu.VMEM((NZ, 16, cols), BF16),
            pltpu.VMEM((2, 16, cols), BF16),
        ]

    return pl.pallas_call(
        gather_reduce,
        out_shape=(
            pltpu.VMEM((2, 16, BLK, BLK), BF16),
            pltpu.VMEM((2, 192, BLK), BF16),
            pltpu.VMEM((2, 128, 128), BF16),
        ),
        in_specs=[hbm] * 3,
        out_specs=(vmem, vmem, vmem),
        scratch_shapes=[
            pltpu.VMEM((16, 512, BLK), BF16),
            pltpu.VMEM((16, 512, BLK), BF16),
            pltpu.VMEM((512, BLK), F32),
            pltpu.VMEM((BLK, 512), BF16),
            pltpu.VMEM((16, BLK, BLK), BF16),
            *run_buffers(48, BLK, 12),
            *run_buffers(16, 128, 8),
            pltpu.SemaphoreType.REGULAR((5,)),
            dma((3,)),
            dma((2,)),
            dma((2,)),
            dma((1,)),
            dma((13,)),
            dma((2,)),
            dma((2, 6)),
            dma((2, 15)),
            dma((2, 2)),
            dma((2, 2)),
            dma((2, 2)),
            dma((2, 2)),
        ],
        compiler_params=pltpu.CompilerParams(
            collective_id=1, has_side_effects=True, vmem_limit_bytes=32 << 20
        ),
        name="gather_and_sum",
    )(acts, cotangent, projector)


def update_kernel(p, g_big, g_small, m1, m2, first_new, second_new, update, first_v, second_v, dir_t, update_v, sems):
    core = lax.axis_index("dp") % 2
    fs = lax.axis_index("fsdp")
    x, y_lo = fs // NYL, fs % NYL
    first_fix = 1.0 - 0.9**STEP
    second_fix = 1.0 - 0.999**STEP
    for half in range(2):
        small = g_small[half]
        low = jnp.concatenate(
            [g_big[half], jnp.concatenate([small[:64], small[64:]], axis=1)], axis=0
        ).astype(F32).T
        which = core if half == 0 else 1 - core
        cols = pl.ds(pl.multiple_of(which * BLK, BLK), BLK)
        first = 0.9 * m1[:, cols] + 0.1 * low
        second = 0.999 * m2[:, cols] + 0.001 * low * low
        first_v[:, cols] = first
        second_v[:, cols] = second
        direction = (first / first_fix / (jnp.sqrt(second / second_fix) + 1e-08)).astype(BF16)
        dir_t[half] = direction.T
    moments = [
        pltpu.make_async_copy(first_v, first_new, sems.at[0]),
        pltpu.make_async_copy(second_v, second_new, sems.at[1]),
    ]
    for copy in moments:
        copy.start()
    for s in range(16):
        update_v[s] = jnp.dot(p[0, s], dir_t[0], preferred_element_type=F32) + jnp.dot(
            p[1, s], dir_t[1], preferred_element_type=F32
        )
        block = ((x + s // 4) % NX) * NYL + (y_lo + s % 4) % NYL
        place = pl.ds(pl.multiple_of(block * BLK, BLK), BLK)
        pltpu.make_async_copy(update_v.at[s], update.at[place], sems.at[2]).start()
    for copy in moments:
        copy.wait()
    pltpu.make_async_copy(update_v, update_v, sems.at[2]).wait()


def adam_and_update(p, g_big, g_small, first_moment, second_moment):
    vmem = pl.BlockSpec(memory_space=pltpu.VMEM)
    return pl.pallas_call(
        update_kernel,
        out_shape=(
            jax.ShapeDtypeStruct((BLK, 512), F32),
            jax.ShapeDtypeStruct((BLK, 512), F32),
            jax.ShapeDtypeStruct((4096, BLK), F32),
        ),
        in_specs=[vmem] * 5,
        out_specs=(pl.BlockSpec(memory_space=pl.ANY),) * 3,
        scratch_shapes=[
            pltpu.VMEM((BLK, 512), F32),
            pltpu.VMEM((BLK, 512), F32),
            pltpu.VMEM((2, BLK, BLK), BF16),
            pltpu.VMEM((16, BLK, BLK), F32),
            pltpu.SemaphoreType.DMA((3,)),
        ],
        compiler_params=pltpu.CompilerParams(vmem_limit_bytes=40 << 20),
        name="adam_and_update",
    )(p, g_big, g_small, first_moment, second_moment)


def on_device(acts, cotangent, projector, first_moment, second_moment):
    p, g_big, g_small = gather_and_sum(
        *(pltpu.with_memory_space_constraint(a, pltpu.HBM) for a in (acts, cotangent, projector))
    )
    return adam_and_update(p, g_big, g_small, first_moment, second_moment)


def solution(mesh):
    in_specs = (
        P(("dp", "fsdp"), None),
        P(("dp", "fsdp"), None),
        P("fsdp", None),
        P("fsdp", None),
        P("fsdp", None),
    )
    out_specs = (P("fsdp", None), P("fsdp", None), P(None, "fsdp"))
    return jax.shard_map(
        on_device, mesh=mesh, in_specs=in_specs, out_specs=out_specs, check_vma=False
    )
```

```python
import jax
import jax.numpy as jnp
from jax import lax
from jax.experimental import pallas as pl
from jax.experimental.pallas import tpu as pltpu
from jax.sharding import PartitionSpec as P

MESH = pl.DeviceIdType.MESH
STEP = 2
NX, NY, NYL, NZ = 4, 8, 4, 12
BLK = 256
HALF, QUART = 128, 64
X, Y = 0, 1
BF16, F32 = jnp.bfloat16, jnp.float32


def gather_reduce(
    acts, cot, proj, p_v, g_v,
    acts_v, cot_v, acc, coords_t, term_v,
    far1a, dir1a, comb1a, csrc1a, mid_a, own2a, far2a, dir2a, comb2a, csrc2a, zb_a, zrecv_a, ybuf_a,
    far1b, dir1b, comb1b, csrc1b, mid_b, own2b, far2b, dir2b, comb2b, csrc2b, zb_b, zrecv_b, ybuf_b,
    hello, ld_sem, sib_send, sib_recv, ag_send, ag_recv, osib_sem,
    rs_send, rs_recv, z_sem, y_sem, g_sem, fin_sem,
):
    dp, fs = lax.axis_index("dp"), lax.axis_index("fsdp")
    core, y_hi, z = dp % 2, (dp // 2) % 2, dp // 4
    x, y_lo = fs // NYL, fs % NYL
    y = y_hi * NYL + y_lo

    def device(dx=0, dy=0, dz=0, other=False):
        yy = (y + dy + NY) % NY
        xx = (x + dx + NX) % NX
        zz = (z + dz) % NZ
        cc = 1 - core if other else core
        return ((zz * 2 + yy // NYL) * 2 + cc, xx * NYL + yy % NYL)

    sibling = device(other=True)
    near = {(X, 1): device(dx=1), (X, -1): device(dx=-1), (Y, 1): device(dy=1), (Y, -1): device(dy=-1)}
    across = device(dy=4)
    column = [device(dz=k) for k in range(NZ)]
    mine = pl.ds(pl.multiple_of(core * BLK, BLK), BLK)
    ranks = [pl.ds(c * HALF, HALF) for c in (0, 1)]

    def columns(s):
        block = ((x + s // 4) % NX) * NYL + (y_lo + s % 4) % NYL
        return pl.ds(pl.multiple_of(block * BLK, BLK), BLK)

    def load(s, _):
        pltpu.make_async_copy(acts.at[:, columns(s)], acts_v.at[s, pl.ds(0, BLK)], ld_sem.at[0]).start()
        pltpu.make_async_copy(cot.at[:, columns(s)], cot_v.at[s, pl.ds(0, BLK)], ld_sem.at[1]).start()
        return 0

    barrier = pltpu.get_barrier_semaphore()
    peers = [*near.values(), column[1], column[NZ - 1], sibling]
    for peer in peers:
        pl.semaphore_signal(barrier, inc=1, device_id=peer, device_id_type=MESH)
    own_p = pltpu.make_async_copy(proj.at[:, mine], p_v.at[0, 0], ld_sem.at[2])
    own_p.start()
    acc[...] = jnp.zeros_like(acc)
    pl.semaphore_wait(barrier, len(peers))

    chain = [near[Y, 1], near[Y, -1], column[1], column[NZ - 1]]

    def greet(r):
        if r > 0:
            pl.semaphore_wait(hello.at[r - 1], len(chain))
        if r < 5:
            for peer in chain:
                pl.semaphore_signal(hello.at[r], inc=1, device_id=peer, device_id_type=MESH)

    def remote(src, dst, send, recv, target):
        copy = pltpu.make_async_remote_copy(
            src_ref=src, dst_ref=dst, send_sem=send, recv_sem=recv, device_id=target, device_id_type=MESH
        )
        copy.start()
        return copy

    def arrived(ref, sem):
        pltpu.make_async_copy(ref, ref, sem).wait()

    both = (3, 0), (1, 0), (2, 0), (0, 3), (0, 1), (3, 3), (3, 1), (1, 3), (1, 1), (2, 3), (2, 1)

    def group(u, v):
        u, v = u % 4, v % 4
        return both.index((u, v)) if (u, v) in both else len(both) + (u == 2)

    def slot(part, u, v):
        return (u % 4) * 4 + v % 4 if part == 0 else (v % 4) * 4 + u % 4

    def rows(part, half):
        if half is None:
            return pl.ds(part * HALF, HALF)
        return pl.ds(part * HALF + half * QUART, QUART)

    class Gather:
        def __init__(self, c):
            self.c, self.seen = c, set()

        def spread(self, part, u, v, half, stage, way):
            axis = (X, Y)[part] if stage == 1 else (Y, X)[part]
            s = slot(part, u, v)
            at = (u - way, v) if stage == 1 else (u, v - way)
            r = rows(part, half)
            if s == 0:
                src = proj.at[r, pl.ds(pl.multiple_of(core * BLK + self.c * HALF, HALF), HALF)]
            else:
                src = p_v.at[0, s, r, ranks[self.c]]
            dst = p_v.at[0, slot(part, *at), r, ranks[self.c]]
            remote(src, dst, ag_send.at[self.c], ag_recv.at[self.c, group(*at)], near[axis, way])

        def gotten(self, u, v):
            if (u % 4, v % 4) == (0, 0):
                return
            g = group(u, v)
            if g not in self.seen:
                self.seen.add(g)
                n = 3 if g == len(both) else 1
                arrived(p_v.at[0, pl.ds(0, n), :, ranks[self.c]], ag_recv.at[self.c, g])

        def own(self):
            for stage in (1, 2):
                for part in (0, 1):
                    for way in (1, -1):
                        self.spread(part, 0, 0, None, stage, way)

        def beside(self):
            for u, half, way in ((3, 0, 1), (1, 1, -1)):
                self.gotten(u, 0)
                for part in (0, 1):
                    self.spread(part, u, 0, half, 1, way)
            for part in (0, 1):
                for u in (3, 1):
                    self.spread(part, u, 0, None, 2, 1)
                    self.spread(part, u, 0, None, 2, -1)

        def relay(self, u):
            for v, half, way in ((3, 0, 1), (1, 1, -1)):
                self.gotten(u, v)
                for part in (0, 1):
                    self.spread(part, u, v, half, 2, way)

        def opposite(self):
            self.gotten(2, 0)
            for part in (0, 1):
                self.spread(part, 2, 0, None, 2, 1)
                self.spread(part, 2, 0, None, 2, -1)

        def multiply(self, *places):
            for rx, ry in places:
                s = (rx % 4) * 4 + ry % 4
                self.gotten(rx, ry)
                self.gotten(ry, rx)
                acc[self.c] += jnp.dot(acts_v[s], p_v[0, s, :, ranks[self.c]], preferred_element_type=F32)

        def finish(self):
            coords_t[self.c] = acc[self.c].astype(BF16).T

    def lend(s, _):
        remote(acts.at[:, columns(s)], acts_v.at[s, pl.ds(BLK, BLK)], sib_send.at[0], sib_recv.at[0], sibling)
        return 0

    def lend_cot(s, _):
        remote(cot.at[:, columns(s)], cot_v.at[s, pl.ds(BLK, BLK)], sib_send.at[1], sib_recv.at[1], sibling)
        return 0

    def give(s, _):
        remote(p_v.at[0, s], p_v.at[1, s], osib_sem.at[0], osib_sem.at[1], sibling)
        return 0

    first = ((Y, X), (X, Y))
    WAYS = ((0, 1), (1, -1))
    order = (2, 1, 3, 0)

    def rs_slot(part, u, v):
        return (v % 4) * 4 + u % 4 if part == 0 else (u % 4) * 4 + v % 4

    class Run:
        def __init__(self, index, low, q, buffers):
            self.pieces = 4 if index else 8
            self.piece_rows = HALF // self.pieces
            self.index, self.low, self.q, self.seen, self.done = index, low, q, set(), set()
            (
                self.far1, self.dir1, self.comb1, self.csrc1, self.mid, self.own2,
                self.far2, self.dir2, self.comb2, self.csrc2, self.zb, self.zrecv, self.ybuf,
            ) = buffers

        def send(self, src, dst, kind, v, axis, way):
            recv = rs_recv.at[self.index, kind * 4 + v if kind < 3 else 9 + kind]
            remote(src, dst, rs_send.at[self.index, kind], recv, near[axis, way])

        def came(self, kind, v=None):
            if (kind, v) in self.seen:
                return
            self.seen.add((kind, v))
            buffer = (self.far1, self.dir1, self.comb1, self.far2, self.dir2, self.comb2)[kind]
            if kind < 3:
                arrived(buffer.at[:, :, v], rs_recv.at[self.index, kind * 4 + v])
            else:
                arrived(buffer, rs_recv.at[self.index, 9 + kind])

        def need(self, part, u, v):
            s = rs_slot(part, u, v)
            if s not in self.done:
                self.done.add(s)
                term_v[s, ranks[self.index], :] = jnp.dot(
                    coords_t[self.index], cot_v[s], preferred_element_type=F32
                ).astype(BF16)
            return s

        def rows(self, part, half):
            return pl.ds(self.low + (2 * part + half) * self.q, self.q)

        def half(self, w):
            return pl.ds(w * self.q, self.q)

        def far(self):
            for v in order:
                for part in (0, 1):
                    s = self.need(part, 2, v)
                    for w, way in WAYS:
                        self.send(
                            term_v.at[s, self.rows(part, w)], self.far1.at[part, w, v],
                            0, v, first[part][0], way,
                        )

        def direct(self):
            for v in order:
                for part in (0, 1):
                    for w, way in WAYS:
                        s = self.need(part, way, v)
                        self.send(
                            term_v.at[s, self.rows(part, 1 - w)], self.dir1.at[part, w, v],
                            1, v, first[part][0], way,
                        )

        def combine(self):
            for v in order:
                for part in (0, 1):
                    for w, way in WAYS:
                        s = rs_slot(part, way, v)
                        self.came(0, v)
                        self.csrc1[part, w, v] = (
                            term_v[s, self.rows(part, w), :].astype(F32) + self.far1[part, w, v].astype(F32)
                        ).astype(BF16)
                        self.send(
                            self.csrc1.at[part, w, v], self.comb1.at[part, w, v],
                            2, v, first[part][0], way,
                        )

        def total1(self, part, v, w):
            s = rs_slot(part, 0, v)
            self.came(2, v)
            self.came(1, v)
            return (
                term_v[s, self.rows(part, w), :].astype(F32)
                + self.comb1[part, w, v].astype(F32)
                + self.dir1[part, 1 - w, v].astype(F32)
            )

        def middle(self):
            for v in (2, 1, 3):
                for part in (0, 1):
                    for w, way in WAYS:
                        self.mid[part, v, self.half(w), :] = self.total1(part, v, w).astype(BF16)
                        src = self.mid.at[part, v, self.half(w)]
                        if v == 2:
                            self.send(
                                src, self.far2.at[part, w], 3, 0, first[part][1], way
                            )
                        elif v % 4 == (-way) % 4:
                            self.send(
                                src, self.dir2.at[part, 1 - w], 4, 0, first[part][1], -way
                            )

        def own(self):
            for part in (0, 1):
                for w, _ in WAYS:
                    self.own2[part, self.half(w), :] = self.total1(part, 0, w)

        def combine2(self):
            for part in (0, 1):
                for w, way in WAYS:
                    self.came(3)
                    self.csrc2[part, w] = (
                        self.mid[part, way % 4, self.half(w), :].astype(F32) + self.far2[part, w].astype(F32)
                    ).astype(BF16)
                    self.send(
                        self.csrc2.at[part, w], self.comb2.at[part, w], 5, 0, first[part][1], way
                    )

        def total2(self):
            for part in (0, 1):
                for w, _ in WAYS:
                    self.came(5)
                    self.came(4)
                    total = (
                        self.own2[part, self.half(w), :]
                        + self.comb2[part, w].astype(F32)
                        + self.dir2[part, 1 - w].astype(F32)
                    ).astype(BF16)
                    at = (2 * part + w) * self.q
                    self.zb[pl.ds(at, self.q), :] = total

    run0 = Run(
        0, 0, 32,
        (far1a, dir1a, comb1a, csrc1a, mid_a, own2a, far2a, dir2a, comb2a, csrc2a, zb_a, zrecv_a, ybuf_a),
    )
    run1 = Run(
        1, 128, 32,
        (far1b, dir1b, comb1b, csrc1b, mid_b, own2b, far2b, dir2b, comb2b, csrc2b, zb_b, zrecv_b, ybuf_b),
    )

    far_first = (6, 5, 7, 4, 8, 3, 9, 2, 10, 1, 11)

    def piece(run, k, base=0):
        zz = (z + k) % NZ
        index = zz // 3 * 2 + zz % 3 if run.index == 0 else (zz + 2) % NZ
        return pl.ds(pl.multiple_of(base + index * run.piece_rows, 16), run.piece_rows)

    def sums(run, k=0):
        zz = (z + k) % NZ
        return zz % 3 != 2 if run.index == 0 else (zz + 2) % NZ < 4

    def owned(run, k, body):
        pl.when(sums(run, k))(body)

    def scatter(run):
        for k in far_first:

            def body(k=k):
                remote(run.zb.at[piece(run, k)], run.zrecv.at[k], z_sem.at[run.index, 0], z_sem.at[run.index, 1], column[k])

            owned(run, k, body)

    def swap(run):
        def body():
            part_sum = run.zb[piece(run, 0), :].astype(F32)
            arrived(run.zrecv.at[pl.ds(1, NZ - 1)], z_sem.at[run.index, 1])
            for k in range(1, NZ):
                part_sum += run.zrecv[k].astype(F32)
            run.ybuf[0] = part_sum.astype(BF16)
            remote(run.ybuf.at[0], run.ybuf.at[1], y_sem.at[run.index, 0], y_sem.at[run.index, 1], across)

        owned(run, 0, body)

    def settle(run):
        def body():
            arrived(run.ybuf.at[1], y_sem.at[run.index, 1])
            g_v[0, piece(run, 0, run.low), :] = (run.ybuf[0].astype(F32) + run.ybuf[1].astype(F32)).astype(BF16)

        owned(run, 0, body)

    def hand_out(run, places):
        def body():
            at = piece(run, 0, run.low)
            for place in places:

                @pl.when(z != place)
                def _():
                    remote(
                        g_v.at[0, at], g_v.at[0, at], g_sem.at[run.index, 0], g_sem.at[run.index, 1],
                        ((place * 2 + y_hi) * 2 + core, fs),
                    )

        owned(run, 0, body)

    def others(run, body):
        pl.when(sums(run))(lambda: body(run.pieces - 1))
        pl.when(jnp.logical_not(sums(run)))(lambda: body(run.pieces))

    def collect(run):
        others(run, lambda n: arrived(run.zrecv.at[pl.ds(0, n)], g_sem.at[run.index, 1]))
        span = pl.ds(run.low, 4 * run.q)
        return remote(g_v.at[0, span], g_v.at[1, span], fin_sem.at[run.index, 0], fin_sem.at[run.index, 1], sibling)

    gather0, gather1 = Gather(0), Gather(1)
    SIDES = ((1, 0), (3, 0), (0, 1), (0, 3))
    CORNERS = ((2, 0), (0, 2), (1, 1), (1, 3), (3, 1), (3, 3))
    LAST = ((1, 2), (3, 2), (2, 1), (2, 3), (2, 2))
    gather0.own()
    lax.fori_loop(0, 16, load, 0)
    greet(0)
    lax.fori_loop(0, 16, lend, 0)
    own_p.wait()
    gather0.beside()
    gather1.own()
    gather0.relay(0)
    greet(1)
    gather0.opposite()
    lax.fori_loop(0, 16, lend_cot, 0)
    gather1.beside()
    gather0.relay(3)
    gather0.relay(1)
    arrived(acts_v.at[:, pl.ds(0, BLK)], ld_sem.at[0])
    arrived(acts_v.at[:, pl.ds(BLK, BLK)], sib_recv.at[0])
    gather0.multiply((0, 0), *SIDES)
    gather1.relay(0)
    greet(2)
    gather0.relay(2)
    gather1.opposite()
    gather0.multiply(*CORNERS)
    greet(3)
    gather0.multiply(*LAST)
    gather0.finish()
    gather1.relay(3)
    gather1.relay(1)
    arrived(cot_v.at[:, pl.ds(0, BLK)], ld_sem.at[1])
    arrived(cot_v.at[:, pl.ds(BLK, BLK)], sib_recv.at[1])
    run0.far()
    gather1.relay(2)
    run0.direct()
    run0.need(0, 0, 0)
    greet(4)
    gather1.multiply((0, 0), *SIDES, *CORNERS)
    run0.combine()
    gather1.multiply(*LAST)
    gather1.finish()
    run1.far()
    greet(5)
    run0.middle()
    run1.direct()
    run1.need(0, 0, 0)
    run0.own()
    run0.combine2()
    run1.combine()
    run0.total2()
    scatter(run0)
    run1.middle()
    lax.fori_loop(0, 16, give, 0)
    run1.own()
    run1.combine2()
    run1.total2()
    scatter(run1)
    places = (0, 1, 2, 3, 4, 5, 11, 10, 9, 8, 7, 6)
    for run in (run0, run1):
        swap(run)
        settle(run)
        hand_out(run, places)
    tell = [collect(run0), collect(run1)]

    arrived(acts_v.at[:, pl.ds(0, BLK)], sib_send.at[0])
    arrived(cot_v.at[:, pl.ds(0, BLK)], sib_send.at[1])
    arrived(p_v.at[0], osib_sem.at[0])
    arrived(p_v.at[1], osib_sem.at[1])
    for c in (0, 1):
        arrived(p_v.at[0, pl.ds(0, 15), :, ranks[c]], ag_send.at[c])
    for run in (run0, run1):
        for kind, buffer in enumerate((run.far1, run.dir1, run.comb1, run.far2, run.dir2, run.comb2)):
            arrived(buffer, rs_send.at[run.index, kind])
        others(run, lambda n, run=run: arrived(run.zrecv.at[pl.ds(0, n)], z_sem.at[run.index, 0]))

        def body(run=run):
            arrived(run.ybuf.at[0], y_sem.at[run.index, 0])
            arrived(run.zrecv.at[pl.ds(0, NZ - 1)], g_sem.at[run.index, 0])

        owned(run, 0, body)
    for copy in tell:
        copy.wait()


def gather_and_sum(acts, cotangent, projector):
    dma = pltpu.SemaphoreType.DMA
    hbm = pl.BlockSpec(memory_space=pltpu.HBM)
    vmem = pl.BlockSpec(memory_space=pltpu.VMEM)

    def run_buffers(q, piece_rows):
        first_stage = [pltpu.VMEM((2, 2, 4, q, BLK), BF16)] * 4
        second_stage = [pltpu.VMEM((2, 2, q, BLK), BF16)] * 4
        return [
            *first_stage,
            pltpu.VMEM((2, 4, 2 * q, BLK), BF16),
            pltpu.VMEM((2, 2 * q, BLK), F32),
            *second_stage,
            pltpu.VMEM((4 * q, BLK), BF16),
            pltpu.VMEM((NZ, piece_rows, BLK), BF16),
            pltpu.VMEM((2, piece_rows, BLK), BF16),
        ]

    return pl.pallas_call(
        gather_reduce,
        out_shape=(
            pltpu.VMEM((2, 16, BLK, BLK), BF16),
            pltpu.VMEM((2, BLK, BLK), BF16),
        ),
        in_specs=[hbm] * 3,
        out_specs=(vmem, vmem),
        scratch_shapes=[
            pltpu.VMEM((16, 512, BLK), BF16),
            pltpu.VMEM((16, 512, BLK), BF16),
            pltpu.VMEM((2, 512, HALF), F32),
            pltpu.VMEM((2, HALF, 512), BF16),
            pltpu.VMEM((16, BLK, BLK), BF16),
            *run_buffers(32, 16),
            *run_buffers(32, 32),
            pltpu.SemaphoreType.REGULAR((5,)),
            dma((3,)),
            dma((2,)),
            dma((2,)),
            dma((2,)),
            dma((2, 13)),
            dma((2,)),
            dma((2, 6)),
            dma((2, 15)),
            dma((2, 2)),
            dma((2, 2)),
            dma((2, 2)),
            dma((2, 2)),
        ],
        compiler_params=pltpu.CompilerParams(
            collective_id=1, has_side_effects=True, vmem_limit_bytes=32 << 20
        ),
        name="gather_and_sum",
    )(acts, cotangent, projector)


def update_kernel(p, g_v, m1, m2, first_new, second_new, update, first_v, second_v, dir_t, update_v, sems):
    core = lax.axis_index("dp") % 2
    fs = lax.axis_index("fsdp")
    x, y_lo = fs // NYL, fs % NYL
    first_fix = 1.0 - 0.9**STEP
    second_fix = 1.0 - 0.999**STEP
    for half in range(2):
        low = g_v[half].astype(F32).T
        which = core if half == 0 else 1 - core
        cols = pl.ds(pl.multiple_of(which * BLK, BLK), BLK)
        first = 0.9 * m1[:, cols] + 0.1 * low
        second = 0.999 * m2[:, cols] + 0.001 * low * low
        first_v[:, cols] = first
        second_v[:, cols] = second
        direction = (first / first_fix / (jnp.sqrt(second / second_fix) + 1e-08)).astype(BF16)
        dir_t[half] = direction.T
    moments = [
        pltpu.make_async_copy(first_v, first_new, sems.at[0]),
        pltpu.make_async_copy(second_v, second_new, sems.at[1]),
    ]
    for copy in moments:
        copy.start()
    for s in range(16):
        update_v[s] = jnp.dot(p[0, s], dir_t[0], preferred_element_type=F32) + jnp.dot(
            p[1, s], dir_t[1], preferred_element_type=F32
        )
        block = ((x + s // 4) % NX) * NYL + (y_lo + s % 4) % NYL
        place = pl.ds(pl.multiple_of(block * BLK, BLK), BLK)
        pltpu.make_async_copy(update_v.at[s], update.at[place], sems.at[2]).start()
    for copy in moments:
        copy.wait()
    pltpu.make_async_copy(update_v, update_v, sems.at[2]).wait()


def adam_and_update(p, g_v, first_moment, second_moment):
    vmem = pl.BlockSpec(memory_space=pltpu.VMEM)
    return pl.pallas_call(
        update_kernel,
        out_shape=(
            jax.ShapeDtypeStruct((BLK, 512), F32),
            jax.ShapeDtypeStruct((BLK, 512), F32),
            jax.ShapeDtypeStruct((4096, BLK), F32),
        ),
        in_specs=[vmem] * 4,
        out_specs=(pl.BlockSpec(memory_space=pl.ANY),) * 3,
        scratch_shapes=[
            pltpu.VMEM((BLK, 512), F32),
            pltpu.VMEM((BLK, 512), F32),
            pltpu.VMEM((2, BLK, BLK), BF16),
            pltpu.VMEM((16, BLK, BLK), F32),
            pltpu.SemaphoreType.DMA((3,)),
        ],
        compiler_params=pltpu.CompilerParams(vmem_limit_bytes=40 << 20),
        name="adam_and_update",
    )(p, g_v, first_moment, second_moment)


def on_device(acts, cotangent, projector, first_moment, second_moment):
    p, g_v = gather_and_sum(
        *(pltpu.with_memory_space_constraint(a, pltpu.HBM) for a in (acts, cotangent, projector))
    )
    return adam_and_update(p, g_v, first_moment, second_moment)


def solution(mesh):
    in_specs = (
        P(("dp", "fsdp"), None),
        P(("dp", "fsdp"), None),
        P("fsdp", None),
        P("fsdp", None),
        P("fsdp", None),
    )
    out_specs = (P("fsdp", None), P("fsdp", None), P(None, "fsdp"))
    return jax.shard_map(
        on_device, mesh=mesh, in_specs=in_specs, out_specs=out_specs, check_vma=False
    )
```

```python
import jax
import jax.numpy as jnp
from jax import lax
from jax.experimental import pallas as pl
from jax.experimental.pallas import tpu as pltpu
from jax.sharding import PartitionSpec as P

MESH = pl.DeviceIdType.MESH
STEP = 2
NX, NY, NYL, NZ = 4, 8, 4, 12
BLK = 256
HALF, QUART = 128, 64
X, Y = 0, 1
BF16, F32 = jnp.bfloat16, jnp.float32


def gather_reduce(
    acts, cot, proj, p_v, g_v,
    acts_v, cot_v, acc, coords_t, term_v,
    far1a, dir1a, comb1a, csrc1a, mid_a, own2a, far2a, dir2a, comb2a, csrc2a, zb_a, zrecv_a, ybuf_a,
    far1b, dir1b, comb1b, csrc1b, mid_b, own2b, far2b, dir2b, comb2b, csrc2b, zb_b, zrecv_b, ybuf_b,
    hello, ld_sem, sib_send, sib_recv, ag_send, ag_recv, osib_sem,
    rs_send, rs_recv, z_sem, y_sem, g_sem, fin_sem,
):
    dp, fs = lax.axis_index("dp"), lax.axis_index("fsdp")
    core, y_hi, z = dp % 2, (dp // 2) % 2, dp // 4
    x, y_lo = fs // NYL, fs % NYL
    y = y_hi * NYL + y_lo

    def device(dx=0, dy=0, dz=0, other=False):
        yy = (y + dy + NY) % NY
        xx = (x + dx + NX) % NX
        zz = (z + dz) % NZ
        cc = 1 - core if other else core
        return ((zz * 2 + yy // NYL) * 2 + cc, xx * NYL + yy % NYL)

    sibling = device(other=True)
    near = {(X, 1): device(dx=1), (X, -1): device(dx=-1), (Y, 1): device(dy=1), (Y, -1): device(dy=-1)}
    across = device(dy=4)
    column = [device(dz=k) for k in range(NZ)]
    mine = pl.ds(pl.multiple_of(core * BLK, BLK), BLK)
    ranks = [pl.ds(c * HALF, HALF) for c in (0, 1)]

    def columns(s):
        block = ((x + s // 4) % NX) * NYL + (y_lo + s % 4) % NYL
        return pl.ds(pl.multiple_of(block * BLK, BLK), BLK)

    def load(s, _):
        pltpu.make_async_copy(acts.at[:, columns(s)], acts_v.at[s, pl.ds(0, BLK)], ld_sem.at[0]).start()
        pltpu.make_async_copy(cot.at[:, columns(s)], cot_v.at[s, pl.ds(0, BLK)], ld_sem.at[1]).start()
        return 0

    barrier = pltpu.get_barrier_semaphore()
    peers = [*near.values(), column[1], column[NZ - 1], sibling]
    for peer in peers:
        pl.semaphore_signal(barrier, inc=1, device_id=peer, device_id_type=MESH)
    own_p = pltpu.make_async_copy(proj.at[:, mine], p_v.at[0, 0], ld_sem.at[2])
    own_p.start()
    acc[...] = jnp.zeros_like(acc)
    pl.semaphore_wait(barrier, len(peers))

    chain = [near[Y, 1], near[Y, -1], column[1], column[NZ - 1]]

    def greet(r):
        if r > 0:
            pl.semaphore_wait(hello.at[r - 1], len(chain))
        if r < 5:
            for peer in chain:
                pl.semaphore_signal(hello.at[r], inc=1, device_id=peer, device_id_type=MESH)

    def remote(src, dst, send, recv, target):
        copy = pltpu.make_async_remote_copy(
            src_ref=src, dst_ref=dst, send_sem=send, recv_sem=recv, device_id=target, device_id_type=MESH
        )
        copy.start()
        return copy

    def arrived(ref, sem):
        pltpu.make_async_copy(ref, ref, sem).wait()

    both = (3, 0), (1, 0), (2, 0), (0, 3), (0, 1), (3, 3), (3, 1), (1, 3), (1, 1), (2, 3), (2, 1)

    def group(u, v):
        u, v = u % 4, v % 4
        return both.index((u, v)) if (u, v) in both else len(both) + (u == 2)

    def slot(part, u, v):
        return (u % 4) * 4 + v % 4 if part == 0 else (v % 4) * 4 + u % 4

    def rows(part, half):
        if half is None:
            return pl.ds(part * HALF, HALF)
        return pl.ds(part * HALF + half * QUART, QUART)

    class Gather:
        def __init__(self, c):
            self.c, self.seen = c, set()

        def spread(self, part, u, v, half, stage, way):
            axis = (X, Y)[part] if stage == 1 else (Y, X)[part]
            s = slot(part, u, v)
            at = (u - way, v) if stage == 1 else (u, v - way)
            r = rows(part, half)
            if s == 0:
                src = proj.at[r, pl.ds(pl.multiple_of(core * BLK + self.c * HALF, HALF), HALF)]
            else:
                src = p_v.at[0, s, r, ranks[self.c]]
            dst = p_v.at[0, slot(part, *at), r, ranks[self.c]]
            remote(src, dst, ag_send.at[self.c], ag_recv.at[self.c, group(*at)], near[axis, way])

        def gotten(self, u, v):
            if (u % 4, v % 4) == (0, 0):
                return
            g = group(u, v)
            if g not in self.seen:
                self.seen.add(g)
                n = 3 if g == len(both) else 1
                arrived(p_v.at[0, pl.ds(0, n), :, ranks[self.c]], ag_recv.at[self.c, g])

        def own(self):
            for stage in (1, 2):
                for part in (0, 1):
                    for way in (1, -1):
                        self.spread(part, 0, 0, None, stage, way)

        def beside(self):
            for u, half, way in ((3, 0, 1), (1, 1, -1)):
                self.gotten(u, 0)
                for part in (0, 1):
                    self.spread(part, u, 0, half, 1, way)
            for part in (0, 1):
                for u in (3, 1):
                    self.spread(part, u, 0, None, 2, 1)
                    self.spread(part, u, 0, None, 2, -1)

        def relay(self, u):
            for v, half, way in ((3, 0, 1), (1, 1, -1)):
                self.gotten(u, v)
                for part in (0, 1):
                    self.spread(part, u, v, half, 2, way)

        def opposite(self):
            self.gotten(2, 0)
            for part in (0, 1):
                self.spread(part, 2, 0, None, 2, 1)
                self.spread(part, 2, 0, None, 2, -1)

        def multiply(self, *places):
            for rx, ry in places:
                s = (rx % 4) * 4 + ry % 4
                self.gotten(rx, ry)
                self.gotten(ry, rx)
                acc[self.c] += jnp.dot(acts_v[s], p_v[0, s, :, ranks[self.c]], preferred_element_type=F32)

        def finish(self):
            coords_t[self.c] = acc[self.c].astype(BF16).T

    def lend(s, _):
        remote(acts.at[:, columns(s)], acts_v.at[s, pl.ds(BLK, BLK)], sib_send.at[0], sib_recv.at[0], sibling)
        return 0

    def lend_cot(s, _):
        remote(cot.at[:, columns(s)], cot_v.at[s, pl.ds(BLK, BLK)], sib_send.at[1], sib_recv.at[1], sibling)
        return 0

    def give(s, _):
        remote(p_v.at[0, s], p_v.at[1, s], osib_sem.at[0], osib_sem.at[1], sibling)
        return 0

    first = ((Y, X), (X, Y))
    WAYS = ((0, 1), (1, -1))
    order = (2, 1, 3, 0)

    def rs_slot(part, u, v):
        return (v % 4) * 4 + u % 4 if part == 0 else (u % 4) * 4 + v % 4

    class Run:
        def __init__(self, index, low, q, buffers):
            self.pieces = 4 if index else 8
            self.piece_rows = HALF // self.pieces
            self.index, self.low, self.q, self.seen, self.done = index, low, q, set(), set()
            (
                self.far1, self.dir1, self.comb1, self.csrc1, self.mid, self.own2,
                self.far2, self.dir2, self.comb2, self.csrc2, self.zb, self.zrecv, self.ybuf,
            ) = buffers

        def send(self, src, dst, kind, v, axis, way):
            recv = rs_recv.at[self.index, kind * 4 + v if kind < 3 else 9 + kind]
            remote(src, dst, rs_send.at[self.index, kind], recv, near[axis, way])

        def came(self, kind, v=None):
            if (kind, v) in self.seen:
                return
            self.seen.add((kind, v))
            buffer = (self.far1, self.dir1, self.comb1, self.far2, self.dir2, self.comb2)[kind]
            if kind < 3:
                arrived(buffer.at[:, :, v], rs_recv.at[self.index, kind * 4 + v])
            else:
                arrived(buffer, rs_recv.at[self.index, 9 + kind])

        def need(self, part, u, v):
            s = rs_slot(part, u, v)
            if s not in self.done:
                self.done.add(s)
                term_v[s, ranks[self.index], :] = jnp.dot(
                    coords_t[self.index], cot_v[s], preferred_element_type=F32
                ).astype(BF16)
            return s

        def rows(self, part, half):
            return pl.ds(self.low + (2 * part + half) * self.q, self.q)

        def half(self, w):
            return pl.ds(w * self.q, self.q)

        def far(self):
            for v in order:
                for part in (0, 1):
                    s = self.need(part, 2, v)
                    for w, way in WAYS:
                        self.send(
                            term_v.at[s, self.rows(part, w)], self.far1.at[part, w, v],
                            0, v, first[part][0], way,
                        )

        def direct(self):
            for v in order:
                for part in (0, 1):
                    for w, way in WAYS:
                        s = self.need(part, way, v)
                        self.send(
                            term_v.at[s, self.rows(part, 1 - w)], self.dir1.at[part, w, v],
                            1, v, first[part][0], way,
                        )

        def combine(self):
            for v in order:
                for part in (0, 1):
                    for w, way in WAYS:
                        s = rs_slot(part, way, v)
                        self.came(0, v)
                        self.csrc1[part, w, v] = (
                            term_v[s, self.rows(part, w), :].astype(F32) + self.far1[part, w, v].astype(F32)
                        ).astype(BF16)
                        self.send(
                            self.csrc1.at[part, w, v], self.comb1.at[part, w, v],
                            2, v, first[part][0], way,
                        )

        def total1(self, part, v, w):
            s = rs_slot(part, 0, v)
            self.came(2, v)
            self.came(1, v)
            return (
                term_v[s, self.rows(part, w), :].astype(F32)
                + self.comb1[part, w, v].astype(F32)
                + self.dir1[part, 1 - w, v].astype(F32)
            )

        def middle(self):
            for v in (2, 1, 3):
                for part in (0, 1):
                    for w, way in WAYS:
                        self.mid[part, v, self.half(w), :] = self.total1(part, v, w).astype(BF16)
                        src = self.mid.at[part, v, self.half(w)]
                        if v == 2:
                            self.send(
                                src, self.far2.at[part, w], 3, 0, first[part][1], way
                            )
                        elif v % 4 == (-way) % 4:
                            self.send(
                                src, self.dir2.at[part, 1 - w], 4, 0, first[part][1], -way
                            )

        def own(self):
            for part in (0, 1):
                for w, _ in WAYS:
                    self.own2[part, self.half(w), :] = self.total1(part, 0, w)

        def combine2(self):
            for part in (0, 1):
                for w, way in WAYS:
                    self.came(3)
                    self.csrc2[part, w] = (
                        self.mid[part, way % 4, self.half(w), :].astype(F32) + self.far2[part, w].astype(F32)
                    ).astype(BF16)
                    self.send(
                        self.csrc2.at[part, w], self.comb2.at[part, w], 5, 0, first[part][1], way
                    )

        def total2(self):
            for part in (0, 1):
                for w, _ in WAYS:
                    self.came(5)
                    self.came(4)
                    total = (
                        self.own2[part, self.half(w), :]
                        + self.comb2[part, w].astype(F32)
                        + self.dir2[part, 1 - w].astype(F32)
                    ).astype(BF16)
                    at = (2 * part + w) * self.q
                    self.zb[pl.ds(at, self.q), :] = total

    run0 = Run(
        0, 0, 32,
        (far1a, dir1a, comb1a, csrc1a, mid_a, own2a, far2a, dir2a, comb2a, csrc2a, zb_a, zrecv_a, ybuf_a),
    )
    run1 = Run(
        1, 128, 32,
        (far1b, dir1b, comb1b, csrc1b, mid_b, own2b, far2b, dir2b, comb2b, csrc2b, zb_b, zrecv_b, ybuf_b),
    )

    far_first = (6, 5, 7, 4, 8, 3, 9, 2, 10, 1, 11)

    def piece(run, k, base=0):
        zz = (z + k) % NZ
        index = zz // 3 * 2 + zz % 3 if run.index == 0 else (zz + 2) % NZ
        return pl.ds(pl.multiple_of(base + index * run.piece_rows, 16), run.piece_rows)

    def sums(run, k=0):
        zz = (z + k) % NZ
        return zz % 3 != 2 if run.index == 0 else (zz + 2) % NZ < 4

    def owned(run, k, body):
        pl.when(sums(run, k))(body)

    def scatter(run):
        for k in far_first:

            def body(k=k):
                remote(run.zb.at[piece(run, k)], run.zrecv.at[k], z_sem.at[run.index, 0], z_sem.at[run.index, 1], column[k])

            owned(run, k, body)

    def swap(run):
        def body():
            part_sum = run.zb[piece(run, 0), :].astype(F32)
            arrived(run.zrecv.at[pl.ds(1, NZ - 1)], z_sem.at[run.index, 1])
            for k in range(1, NZ):
                part_sum += run.zrecv[k].astype(F32)
            run.ybuf[0] = part_sum.astype(BF16)
            remote(run.ybuf.at[0], run.ybuf.at[1], y_sem.at[run.index, 0], y_sem.at[run.index, 1], across)

        owned(run, 0, body)

    def settle(run):
        def body():
            arrived(run.ybuf.at[1], y_sem.at[run.index, 1])
            g_v[0, piece(run, 0, run.low), :] = (run.ybuf[0].astype(F32) + run.ybuf[1].astype(F32)).astype(BF16)

        owned(run, 0, body)

    def hand_out(run, places):
        def body():
            at = piece(run, 0, run.low)
            for place in places:

                @pl.when(z != place)
                def _():
                    remote(
                        g_v.at[0, at], g_v.at[0, at], g_sem.at[run.index, 0], g_sem.at[run.index, 1],
                        ((place * 2 + y_hi) * 2 + core, fs),
                    )

        owned(run, 0, body)

    def others(run, body):
        pl.when(sums(run))(lambda: body(run.pieces - 1))
        pl.when(jnp.logical_not(sums(run)))(lambda: body(run.pieces))

    def collect(run):
        others(run, lambda n: arrived(run.zrecv.at[pl.ds(0, n)], g_sem.at[run.index, 1]))
        span = pl.ds(run.low, 4 * run.q)
        return remote(g_v.at[0, span], g_v.at[1, span], fin_sem.at[run.index, 0], fin_sem.at[run.index, 1], sibling)

    gather0, gather1 = Gather(0), Gather(1)
    SIDES = ((1, 0), (3, 0), (0, 1), (0, 3))
    CORNERS = ((2, 0), (0, 2), (1, 1), (1, 3), (3, 1), (3, 3))
    LAST = ((1, 2), (3, 2), (2, 1), (2, 3), (2, 2))
    gather0.own()
    lax.fori_loop(0, 16, load, 0)
    greet(0)
    lax.fori_loop(0, 16, lend, 0)
    own_p.wait()
    gather0.beside()
    gather1.own()
    gather0.relay(0)
    greet(1)
    gather0.opposite()
    lax.fori_loop(0, 16, lend_cot, 0)
    gather1.beside()
    gather0.relay(3)
    gather0.relay(1)
    arrived(acts_v.at[:, pl.ds(0, BLK)], ld_sem.at[0])
    arrived(acts_v.at[:, pl.ds(BLK, BLK)], sib_recv.at[0])
    gather0.multiply((0, 0), *SIDES)
    gather1.relay(0)
    greet(2)
    gather0.relay(2)
    gather1.opposite()
    gather0.multiply(*CORNERS)
    greet(3)
    gather0.multiply(*LAST)
    gather0.finish()
    gather1.relay(3)
    gather1.relay(1)
    arrived(cot_v.at[:, pl.ds(0, BLK)], ld_sem.at[1])
    arrived(cot_v.at[:, pl.ds(BLK, BLK)], sib_recv.at[1])
    run0.far()
    gather1.relay(2)
    run0.direct()
    run0.need(0, 0, 0)
    greet(4)
    gather1.multiply((0, 0), *SIDES, *CORNERS)
    run0.combine()
    gather1.multiply(*LAST)
    gather1.finish()
    run1.far()
    greet(5)
    run0.middle()
    run1.direct()
    run1.need(0, 0, 0)
    run0.own()
    run0.combine2()
    run1.combine()
    run0.total2()
    scatter(run0)
    run1.middle()
    run1.own()
    run1.combine2()
    run1.total2()
    scatter(run1)
    lax.fori_loop(0, 16, give, 0)
    places = (0, 1, 2, 3, 4, 5, 11, 10, 9, 8, 7, 6)
    for run in (run0, run1):
        swap(run)
        settle(run)
        hand_out(run, places)
    tell = [collect(run0), collect(run1)]

    arrived(acts_v.at[:, pl.ds(0, BLK)], sib_send.at[0])
    arrived(cot_v.at[:, pl.ds(0, BLK)], sib_send.at[1])
    arrived(p_v.at[0], osib_sem.at[0])
    arrived(p_v.at[1], osib_sem.at[1])
    for c in (0, 1):
        arrived(p_v.at[0, pl.ds(0, 15), :, ranks[c]], ag_send.at[c])
    for run in (run0, run1):
        for kind, buffer in enumerate((run.far1, run.dir1, run.comb1, run.far2, run.dir2, run.comb2)):
            arrived(buffer, rs_send.at[run.index, kind])
        others(run, lambda n, run=run: arrived(run.zrecv.at[pl.ds(0, n)], z_sem.at[run.index, 0]))

        def body(run=run):
            arrived(run.ybuf.at[0], y_sem.at[run.index, 0])
            arrived(run.zrecv.at[pl.ds(0, NZ - 1)], g_sem.at[run.index, 0])

        owned(run, 0, body)
    for copy in tell:
        copy.wait()


def gather_and_sum(acts, cotangent, projector):
    dma = pltpu.SemaphoreType.DMA
    hbm = pl.BlockSpec(memory_space=pltpu.HBM)
    vmem = pl.BlockSpec(memory_space=pltpu.VMEM)

    def run_buffers(q, piece_rows):
        first_stage = [pltpu.VMEM((2, 2, 4, q, BLK), BF16)] * 4
        second_stage = [pltpu.VMEM((2, 2, q, BLK), BF16)] * 4
        return [
            *first_stage,
            pltpu.VMEM((2, 4, 2 * q, BLK), BF16),
            pltpu.VMEM((2, 2 * q, BLK), F32),
            *second_stage,
            pltpu.VMEM((4 * q, BLK), BF16),
            pltpu.VMEM((NZ, piece_rows, BLK), BF16),
            pltpu.VMEM((2, piece_rows, BLK), BF16),
        ]

    return pl.pallas_call(
        gather_reduce,
        out_shape=(
            pltpu.VMEM((2, 16, BLK, BLK), BF16),
            pltpu.VMEM((2, BLK, BLK), BF16),
        ),
        in_specs=[hbm] * 3,
        out_specs=(vmem, vmem),
        scratch_shapes=[
            pltpu.VMEM((16, 512, BLK), BF16),
            pltpu.VMEM((16, 512, BLK), BF16),
            pltpu.VMEM((2, 512, HALF), F32),
            pltpu.VMEM((2, HALF, 512), BF16),
            pltpu.VMEM((16, BLK, BLK), BF16),
            *run_buffers(32, 16),
            *run_buffers(32, 32),
            pltpu.SemaphoreType.REGULAR((5,)),
            dma((3,)),
            dma((2,)),
            dma((2,)),
            dma((2,)),
            dma((2, 13)),
            dma((2,)),
            dma((2, 6)),
            dma((2, 15)),
            dma((2, 2)),
            dma((2, 2)),
            dma((2, 2)),
            dma((2, 2)),
        ],
        compiler_params=pltpu.CompilerParams(
            collective_id=1, has_side_effects=True, vmem_limit_bytes=32 << 20
        ),
        name="gather_and_sum",
    )(acts, cotangent, projector)


def update_kernel(p, g_v, m1, m2, first_new, second_new, update, first_v, second_v, dir_t, update_v, sems):
    core = lax.axis_index("dp") % 2
    fs = lax.axis_index("fsdp")
    x, y_lo = fs // NYL, fs % NYL
    first_fix = 1.0 - 0.9**STEP
    second_fix = 1.0 - 0.999**STEP
    for half in range(2):
        low = g_v[half].astype(F32).T
        which = core if half == 0 else 1 - core
        cols = pl.ds(pl.multiple_of(which * BLK, BLK), BLK)
        first = 0.9 * m1[:, cols] + 0.1 * low
        second = 0.999 * m2[:, cols] + 0.001 * low * low
        first_v[:, cols] = first
        second_v[:, cols] = second
        direction = (first / first_fix / (jnp.sqrt(second / second_fix) + 1e-08)).astype(BF16)
        dir_t[half] = direction.T
    moments = [
        pltpu.make_async_copy(first_v, first_new, sems.at[0]),
        pltpu.make_async_copy(second_v, second_new, sems.at[1]),
    ]
    for copy in moments:
        copy.start()
    for s in range(16):
        update_v[s] = jnp.dot(p[0, s], dir_t[0], preferred_element_type=F32) + jnp.dot(
            p[1, s], dir_t[1], preferred_element_type=F32
        )
        block = ((x + s // 4) % NX) * NYL + (y_lo + s % 4) % NYL
        place = pl.ds(pl.multiple_of(block * BLK, BLK), BLK)
        pltpu.make_async_copy(update_v.at[s], update.at[place], sems.at[2]).start()
    for copy in moments:
        copy.wait()
    pltpu.make_async_copy(update_v, update_v, sems.at[2]).wait()


def adam_and_update(p, g_v, first_moment, second_moment):
    vmem = pl.BlockSpec(memory_space=pltpu.VMEM)
    return pl.pallas_call(
        update_kernel,
        out_shape=(
            jax.ShapeDtypeStruct((BLK, 512), F32),
            jax.ShapeDtypeStruct((BLK, 512), F32),
            jax.ShapeDtypeStruct((4096, BLK), F32),
        ),
        in_specs=[vmem] * 4,
        out_specs=(pl.BlockSpec(memory_space=pl.ANY),) * 3,
        scratch_shapes=[
            pltpu.VMEM((BLK, 512), F32),
            pltpu.VMEM((BLK, 512), F32),
            pltpu.VMEM((2, BLK, BLK), BF16),
            pltpu.VMEM((16, BLK, BLK), F32),
            pltpu.SemaphoreType.DMA((3,)),
        ],
        compiler_params=pltpu.CompilerParams(vmem_limit_bytes=40 << 20),
        name="adam_and_update",
    )(p, g_v, first_moment, second_moment)


def on_device(acts, cotangent, projector, first_moment, second_moment):
    p, g_v = gather_and_sum(
        *(pltpu.with_memory_space_constraint(a, pltpu.HBM) for a in (acts, cotangent, projector))
    )
    return adam_and_update(p, g_v, first_moment, second_moment)


def solution(mesh):
    in_specs = (
        P(("dp", "fsdp"), None),
        P(("dp", "fsdp"), None),
        P("fsdp", None),
        P("fsdp", None),
        P("fsdp", None),
    )
    out_specs = (P("fsdp", None), P("fsdp", None), P(None, "fsdp"))
    return jax.shard_map(
        on_device, mesh=mesh, in_specs=in_specs, out_specs=out_specs, check_vma=False
    )
```
